256 devices in a mesh: pair: 16 (over z, x_hi), ctx: 16 (over x_lo, y, core).
Axes of the slice: x: 4 (x_hi: 2, x_lo: 2; x = x_hi * 2 + x_lo), y: 4, z: 8, core: 2. Of those that a mesh axis runs over, the one named last changes fastest.
Arguments:
- queries: bfloat16 [16, 8192, 1024], P('pair', 'ctx'), may hold values from -6 to 6
- keys_values: bfloat16 [16, 8192, 256], P('pair', 'ctx'), may hold values from -6 to 6
- grad_out: bfloat16 [16, 8192, 1024], P('pair', 'ctx'), may hold values from -6 to 6
- log_norms: float32 [16, 8, 8192], P('pair', None, 'ctx'), may hold values from 3 to 8
- out_dots: float32 [16, 8, 8192], P('pair', None, 'ctx'), may hold values from -6 to 6
- doc_ids: int32 [16, 8192], P('pair'), may hold values from 0 to 8191, as said below
Outputs:
- grad_queries: bfloat16 [16, 8192, 1024], P('pair', 'ctx')
- grad_keys_values: bfloat16 [16, 8192, 256], P('pair', 'ctx')
The draws below stay inside these ranges and needn't reach their ends.
Inputs may be any that keep to these rules, and one draw needn't show every extreme that they name: `doc_ids`: in each pack a token's document number is the position of the first token of its document, so numbers never fall along the sequence and each document is a contiguous run; every pack has one of exactly 2048; the last token of every pack is a document of its own; a pack and the pack 16/2 away were matched so that documents of one of them are far longer on average than those of the other.
All inputs are finite; a program needn't handle non-finite values.
Results may differ from the reference program's by a relative error of at most 0.0049.
Values may be sent and summed in bfloat16 or wider, within the bound.
No kernel may reach another device: no remote copies, remote signals or barrier semaphores. Data moves between devices by JAX's collectives and lax.ppermute only.
A program may use at most 128 MiB of HBM per device.

```python
import jax
import jax.numpy as jnp
from jax import lax

H = 8
DH = 128
TOK_DEV = 512
PACKS = 16
SEQ = 8192
SPAN = 2048


def draw_doc_ids(key, part):
    flag_key, cut_key, phase_key = jax.random.split(jax.random.fold_in(key, 7), 3)
    half_flags = jax.random.randint(flag_key, (PACKS // 2, 1), 0, 2)
    pack_flags = jnp.concatenate([half_flags, 1 - half_flags], axis=0)
    cut_draws = jax.random.randint(cut_key, (PACKS, SEQ), 0, SEQ)
    cut_limit = jnp.where(pack_flags == 1, 3, 4 * (SEQ // TOK_DEV))
    phase = jax.random.randint(phase_key, (PACKS, 1), 1, SEQ - SPAN)
    positions = jnp.arange(SEQ, dtype=jnp.int32)[None, :]
    offset = positions - phase
    forced = (offset >= 0) & (jnp.mod(jnp.maximum(offset, 0), SPAN) == 0)
    clean = (offset > 0) & (offset < SPAN)
    doc_starts = ((cut_draws < cut_limit) & jnp.logical_not(clean) | forced).astype(jnp.int32)
    doc_starts = doc_starts.at[:, 0].set(1)
    doc_starts = doc_starts.at[:, SEQ - 1].set(1)
    start_marks = jnp.where(doc_starts == 1, positions, jnp.zeros_like(positions))
    return lax.cummax(start_marks, axis=1).astype(jnp.int32)


def shard_levels(rng, extent, cuts, low, largest):
    level = 1.0
    for position, parts in cuts:
        steps = jax.random.uniform(jax.random.fold_in(jax.random.fold_in(rng, 6), position), (parts,), jnp.float32, low / len(cuts), largest / len(cuts))
        level = level * jnp.repeat(jnp.exp(steps), extent[position] // parts).reshape((-1,) + (1,) * (len(extent) - 1 - position))
    return level


def normal_values(key, extent, scale, limit, shards=(), kind=jnp.bfloat16):
    result = jax.random.normal(key, extent, jnp.float32) * scale
    if len(shards) > 0:
        result = shard_levels(key, extent, shards, -0.22, 0.18) * result
    return jnp.clip(result, min=-limit, max=limit).astype(kind)


def setup_inputs(seed: int = 0) -> dict:
    seeds = jax.random.split(jax.random.key(seed), 7)
    return {
        "queries": normal_values(seeds[0], (PACKS, SEQ, H * DH), 1.0, 6.0, ((0, 16), (1, 16))),
        "keys_values": normal_values(seeds[1], (PACKS, SEQ, 2 * DH), 1.0, 6.0, ((0, 16), (1, 16))),
        "grad_out": normal_values(seeds[2], (PACKS, SEQ, H * DH), 1.0, 6.0, ((0, 16), (1, 16))),
        "log_norms": jnp.clip(3.0 + 5.0 * jax.random.uniform(seeds[3], (PACKS, H, SEQ), jnp.float32) ** shard_levels(seeds[3], (PACKS, H, SEQ), ((0, 16), (2, 16)), -0.2, 0.2), 3.0, 8.0),
        "out_dots": normal_values(seeds[4], (PACKS, H, SEQ), 1.0, 6.0, ((0, 16), (2, 16)), jnp.float32),
        "doc_ids": draw_doc_ids(jax.random.fold_in(seeds[6], 71), 0),
    }


def pack_grads(fields):
    queries, keys_values, grad_out, log_norms, out_dots, doc_row = fields
    head_count = queries.shape[1] // DH
    score_scale = DH ** -0.5
    key_part = keys_values[:, :DH].astype(jnp.float32)
    value_part = keys_values[:, DH:].astype(jnp.float32)
    block_width = min(512, SEQ)
    block_count = SEQ // block_width
    positions = jnp.arange(SEQ, dtype=jnp.int32)

    def advance(totals, index_block):
        first_row = (index_block * block_width).astype(jnp.int32)
        query_block = lax.dynamic_slice_in_dim(queries, first_row, block_width, 0)
        query_block = query_block.reshape(block_width, head_count, DH).astype(jnp.float32)
        cot_block = lax.dynamic_slice_in_dim(grad_out, first_row, block_width, 0)
        cot_block = cot_block.reshape(block_width, head_count, DH).astype(jnp.float32)
        lse_rows = lax.dynamic_slice_in_dim(log_norms, first_row, block_width, 1)
        dot_rows = lax.dynamic_slice_in_dim(out_dots, first_row, block_width, 1)
        query_docs = lax.dynamic_slice_in_dim(doc_row, first_row, block_width, 0)
        query_pos = first_row + jnp.arange(block_width, dtype=jnp.int32)
        allowed = (query_docs[:, None] == doc_row[None, :]) & (positions[None, :] <= query_pos[:, None])
        scores = jnp.einsum("qhd,kd->hqk", query_block, key_part) * score_scale
        probs = jnp.where(allowed[None], jnp.exp(scores - lse_rows[:, :, None]), jnp.float32(0.0))
        prob_grad = jnp.einsum("qhd,kd->hqk", cot_block, value_part)
        score_grad = probs * (prob_grad - dot_rows[:, :, None])
        probs_low = lax.optimization_barrier(probs.astype(jnp.bfloat16)).astype(jnp.float32)
        score_low = lax.optimization_barrier(score_grad.astype(jnp.bfloat16)).astype(jnp.float32)
        query_grad = jnp.einsum("hqk,kd->qhd", score_low, key_part) * score_scale
        key_grad = jnp.einsum("hqk,qhd->kd", score_low, query_block) * score_scale
        value_grad = jnp.einsum("hqk,qhd->kd", probs_low, cot_block)
        totals = totals + jnp.concatenate([key_grad, value_grad], axis=1)
        return totals, query_grad.reshape(block_width, head_count * DH).astype(jnp.bfloat16)

    totals, query_grads = lax.scan(advance, jnp.zeros((SEQ, 2 * DH), jnp.float32), jnp.arange(block_count, dtype=jnp.int32))
    return query_grads.reshape(SEQ, head_count * DH), totals.astype(jnp.bfloat16)


def reference(queries, keys_values, grad_out, log_norms, out_dots, doc_ids):
    grad_queries, grad_keys_values = lax.map(pack_grads, (queries, keys_values, grad_out, log_norms, out_dots, doc_ids))
    return grad_queries, grad_keys_values
```

```python
import functools
import math

import jax
import jax.numpy as jnp
from jax import lax
from jax.experimental import pallas as pl
from jax.experimental.pallas import tpu as pltpu
from jax.sharding import PartitionSpec as P

F32 = jnp.float32
BF16 = jnp.bfloat16
LOG2E = math.log2(math.e)
ROWS = 256
MIB = 1 << 20


def dot(a, b, dim_a, dim_b):
    return lax.dot_general(a, b, (((dim_a,), (dim_b,)), ((), ())), preferred_element_type=F32)


def attend(q, cot, lse, dots, lo, kpos, qpos, kv_ref, kt_ref, acc_ref, dkv_ref, first):
    head_dim = kt_ref.shape[0]
    heads = q.shape[1] // head_dim
    scale = head_dim**-0.5
    keys = kv_ref.shape[0]
    rows = q.shape[0]
    key = kpos + lax.broadcasted_iota(jnp.int32, (keys, rows), 0)
    query = qpos + lax.broadcasted_iota(jnp.int32, (1, rows), 1)
    allowed = (key >= lo) & (key <= query)
    lse2 = lse * LOG2E
    k = kv_ref[:, :head_dim]
    v = kv_ref[:, head_dim:]
    dk = jnp.zeros((keys, head_dim), F32)
    dv = jnp.zeros((keys, head_dim), F32)
    for h in range(heads):
        cols = slice(h * head_dim, (h + 1) * head_dim)
        qh = q[:, cols]
        oh = cot[:, cols]
        scores = dot(k, qh, 1, 1)
        prob_grad = dot(v, oh, 1, 1)
        probs = jnp.where(allowed, jnp.exp2(scores * (scale * LOG2E) - lse2[h : h + 1]), 0.0)
        score_low = (probs * (prob_grad - dots[h : h + 1])).astype(BF16)
        probs_low = probs.astype(BF16)
        dv += dot(probs_low, oh, 1, 0)
        dk += dot(score_low, qh, 1, 0)
        part = dot(kt_ref[...], score_low, 1, 0)
        acc_ref[h] = part if first else acc_ref[h] + part
    dkv_ref[:, :head_dim] += dk * scale
    dkv_ref[:, head_dim:] += dv


def near_kernel(other, place_ref, docs_ref, lo_ref, lse_ref, dots_ref, q_ref, cot_ref, kv_ref, *rest):
    if other:
        dkv_in, _, acc_ref, dkv_ref, kt, acc, sems = rest
    else:
        acc_ref, dkv_ref, kt, acc, sems = rest
    keys = kv_ref.shape[0]
    core = place_ref[1]
    chip_pos = place_ref[0] * (2 * keys)
    kpos = chip_pos + core * keys
    block = 1 - core if other else core
    dkv_ref[...] = dkv_in[...] if other else jnp.zeros_like(dkv_ref)
    kt[...] = kv_ref[:, : kt.shape[0]].T
    per = keys // ROWS
    for g in range(per):
        at = block * per + g
        qpos = pl.multiple_of(chip_pos + at * ROWS, ROWS)
        live = (docs_ref[0, qpos] < kpos + keys) & (qpos + ROWS > kpos)
        rows = slice(g * ROWS, (g + 1) * ROWS)

        @pl.when(live)
        def _():
            attend(q_ref[rows], cot_ref[rows], lse_ref[:, rows], dots_ref[:, rows],
                   lo_ref[0:1, pl.ds(qpos, ROWS)], kpos, qpos, kv_ref, kt, acc.at[g], dkv_ref, True)

        @pl.when(jnp.logical_not(live))
        def _():
            acc[g] = jnp.zeros_like(acc[g])

        pltpu.make_async_copy(acc.at[g], acc_ref.at[at], sems.at[g]).start()
    for g in range(per):
        pltpu.make_async_copy(acc.at[g], acc_ref.at[block * per + g], sems.at[g]).wait()


def far_kernel(chips, place_ref, docs_ref, lo_ref, lse_ref, dots_ref, stat_ref, q_ref, cot_ref,
               q2_ref, cot2_ref, kv_hbm, _, acc_ref, dkv_ref, kv, kt, q, cot, acc, dkv,
               kv_sem, q_sem, cot_sem, in_sem, out_sem):
    keys = kv.shape[0]
    core = place_ref[1]
    chip_pos = place_ref[0] * (2 * keys)
    kpos = (place_ref[0] - chips) * (2 * keys) + core * keys
    per = keys // ROWS
    total = 2 * per
    count = 0
    for g in range(total):
        live = (docs_ref[0, chip_pos + g * ROWS] < kpos + keys) & (kpos >= 0)
        count = count + live.astype(jnp.int32)
    dkv[...] = jnp.zeros_like(dkv)

    def begin(g, unused):
        own = (g // per) == core
        rows = pl.ds(pl.multiple_of((g % per) * ROWS, ROWS), ROWS)

        @pl.when(own)
        def _():
            pltpu.make_async_copy(q_ref.at[rows], q.at[g], q_sem.at[g]).start()
            pltpu.make_async_copy(cot_ref.at[rows], cot.at[g], cot_sem.at[g]).start()

        @pl.when(jnp.logical_not(own))
        def _():
            pltpu.make_async_copy(q2_ref.at[rows], q.at[g], q_sem.at[g]).start()
            pltpu.make_async_copy(cot2_ref.at[rows], cot.at[g], cot_sem.at[g]).start()

        pltpu.make_async_copy(acc_ref.at[g], acc.at[g], in_sem.at[g]).start()
        return unused

    @pl.when(count > 0)
    def _():
        pltpu.make_async_copy(kv_hbm, kv, kv_sem).start()
        lax.fori_loop(0, count, begin, 0)
        pltpu.make_async_copy(kv_hbm, kv, kv_sem).wait()
        kt[...] = kv[:, : kt.shape[0]].T

    def step(g, unused):
        own = (g // per) == core
        cols = pl.ds(pl.multiple_of((g % per) * ROWS, ROWS), ROWS)
        some = pl.ds(0, ROWS)
        pltpu.make_async_copy(q_ref.at[some], q.at[g], q_sem.at[g]).wait()
        pltpu.make_async_copy(cot_ref.at[some], cot.at[g], cot_sem.at[g]).wait()
        pltpu.make_async_copy(acc_ref.at[g], acc.at[g], in_sem.at[g]).wait()
        qpos = pl.multiple_of(chip_pos + g * ROWS, ROWS)
        lse = jnp.where(own, lse_ref[:, cols], stat_ref[0, :, cols])
        dots = jnp.where(own, dots_ref[:, cols], stat_ref[1, :, cols])
        attend(q.at[g], cot.at[g], lse, dots, lo_ref[0:1, pl.ds(qpos, ROWS)], kpos, qpos,
               kv, kt, acc.at[g], dkv, False)
        pltpu.make_async_copy(acc.at[g], acc_ref.at[g], out_sem.at[g]).start()
        return unused

    def end(g, unused):
        pltpu.make_async_copy(acc.at[g], acc_ref.at[g], out_sem.at[g]).wait()
        return unused

    lax.fori_loop(0, count, step, 0)
    dkv_ref[...] = dkv[...].astype(dkv_ref.dtype)
    lax.fori_loop(0, count, end, 0)


def finish_kernel(place_ref, acc_hbm, got_ref, out_ref, acc, sems):
    per, heads, head_dim = got_ref.shape[:3]
    core = place_ref[1]
    scale = head_dim**-0.5
    copies = [
        pltpu.make_async_copy(acc_hbm.at[core * per + g], acc.at[g], sems.at[g]) for g in range(per)
    ]
    for copy in copies:
        copy.start()
    for g in range(per):
        copies[g].wait()
        for h in range(heads):
            part = (acc[g, h] + got_ref[g, h].astype(F32)) * scale
            out_ref[g * ROWS : (g + 1) * ROWS, h * head_dim : (h + 1) * head_dim] = part.T.astype(BF16)


def per_device(chips_ctx, queries, keys_values, grad_out, log_norms, out_dots, doc_ids):
    tok, width = queries.shape[1:]
    head_dim = keys_values.shape[2] // 2
    heads = width // head_dim
    seq = doc_ids.shape[1]
    per = tok // ROWS
    q, kv, cot, lse, dots = queries[0], keys_values[0], grad_out[0], log_norms[0], out_dots[0]
    me = lax.axis_index("ctx")
    place = jnp.stack([me // 2, me % 2]).astype(jnp.int32)
    n_dev = 2 * chips_ctx
    cores = [(i, i ^ 1) for i in range(n_dev)]
    reach = min(chips_ctx - 1, -(-(seq - 2048 - 2) // (2 * tok)))

    q2 = lax.ppermute(q, "ctx", cores)
    cot2 = lax.ppermute(cot, "ctx", cores)
    stat2 = lax.ppermute(jnp.stack([lse, dots]), "ctx", cores)
    far_kv = [
        lax.ppermute(kv, "ctx", [(i, i + 2 * d) for i in range(n_dev - 2 * d)])
        for d in range(1, reach + 1)
    ]

    smem = pl.BlockSpec(memory_space=pltpu.SMEM)
    vmem = pl.BlockSpec(memory_space=pltpu.VMEM)
    hbm = pl.BlockSpec(memory_space=pl.ANY)
    acc_shape = jax.ShapeDtypeStruct((2 * per, heads, head_dim, ROWS), F32)
    tile_flops = 5 * 2 * tok * tok * width
    params = pltpu.CompilerParams(vmem_limit_bytes=40 * MIB)

    def cost(tiles):
        return pl.CostEstimate(flops=int(2 * tiles * tile_flops), bytes_accessed=4 * MIB, transcendentals=0)

    near_scratch = [
        pltpu.VMEM((head_dim, tok), BF16),
        pltpu.VMEM((per, heads, head_dim, ROWS), F32),
        pltpu.SemaphoreType.DMA((per,)),
    ]
    acc, dkv0 = pl.pallas_call(
        functools.partial(near_kernel, False),
        out_shape=(acc_shape, jax.ShapeDtypeStruct((tok, 2 * head_dim), F32)),
        in_specs=[smem, smem] + [vmem] * 6,
        out_specs=(hbm, vmem),
        scratch_shapes=near_scratch,
        compiler_params=params,
        cost_estimate=cost(1),
        name="own_queries",
    )(place, doc_ids, doc_ids, lse, dots, q, cot, kv)
    acc, dkv0 = pl.pallas_call(
        functools.partial(near_kernel, True),
        out_shape=(acc_shape, jax.ShapeDtypeStruct((tok, 2 * head_dim), F32)),
        in_specs=[smem, smem] + [vmem] * 7 + [hbm],
        out_specs=(hbm, vmem),
        scratch_shapes=near_scratch,
        input_output_aliases={9: 0},
        compiler_params=params,
        cost_estimate=cost(1),
        name="other_core",
    )(place, doc_ids, doc_ids, stat2[0], stat2[1], q2, cot2, kv, dkv0, acc)

    sent = []
    for d in range(1, reach + 1):
        acc, part = pl.pallas_call(
            functools.partial(far_kernel, d),
            out_shape=(acc_shape, jax.ShapeDtypeStruct((tok, 2 * head_dim), BF16)),
            in_specs=[smem, smem] + [vmem] * 4 + [hbm] * 6,
            out_specs=(hbm, vmem),
            scratch_shapes=[
                pltpu.VMEM((tok, 2 * head_dim), BF16),
                pltpu.VMEM((head_dim, tok), BF16),
                pltpu.VMEM((2 * per, ROWS, width), BF16),
                pltpu.VMEM((2 * per, ROWS, width), BF16),
                pltpu.VMEM((2 * per, heads, head_dim, ROWS), F32),
                pltpu.VMEM((tok, 2 * head_dim), F32),
                pltpu.SemaphoreType.DMA,
                pltpu.SemaphoreType.DMA((2 * per,)),
                pltpu.SemaphoreType.DMA((2 * per,)),
                pltpu.SemaphoreType.DMA((2 * per,)),
                pltpu.SemaphoreType.DMA((2 * per,)),
            ],
            input_output_aliases={11: 0},
            compiler_params=params,
            cost_estimate=cost(2),
            name=f"back_{d}",
        )(place, doc_ids, doc_ids, lse, dots, stat2, q, cot, q2, cot2, far_kv[d - 1], acc)
        sent.append(lax.ppermute(part, "ctx", [(i + 2 * d, i) for i in range(n_dev - 2 * d)]))

    core = me % 2
    give = lax.dynamic_slice_in_dim(acc, (1 - core) * per, per, 0).astype(BF16)
    got = lax.ppermute(give, "ctx", cores)
    grad_q = pl.pallas_call(
        finish_kernel,
        out_shape=jax.ShapeDtypeStruct((tok, width), BF16),
        in_specs=[smem, hbm, vmem],
        out_specs=vmem,
        scratch_shapes=[
            pltpu.VMEM((per, heads, head_dim, ROWS), F32),
            pltpu.SemaphoreType.DMA((per,)),
        ],
        compiler_params=params,
        name="finish",
    )(place, acc, got)
    grad_kv = dkv0
    for part in sent:
        grad_kv = grad_kv + part.astype(F32)
    return grad_q[None], grad_kv.astype(BF16)[None]


def solution(mesh):
    in_specs = (
        P("pair", "ctx", None),
        P("pair", "ctx", None),
        P("pair", "ctx", None),
        P("pair", None, "ctx"),
        P("pair", None, "ctx"),
        P("pair", None),
    )
    out_specs = (P("pair", "ctx", None), P("pair", "ctx", None))
    return jax.shard_map(
        functools.partial(per_device, mesh.shape["ctx"] // 2),
        mesh=mesh, in_specs=in_specs, out_specs=out_specs, check_vma=False,
    )
```

```python
import functools
import math

import jax
import jax.numpy as jnp
from jax import lax
from jax.experimental import pallas as pl
from jax.experimental.pallas import tpu as pltpu
from jax.sharding import PartitionSpec as P

F32 = jnp.float32
BF16 = jnp.bfloat16
LOG2E = math.log2(math.e)
ROWS = 256
MIB = 1 << 20
SPAN = 2048


def dot(a, b, dim_a, dim_b):
    return lax.dot_general(a, b, (((dim_a,), (dim_b,)), ((), ())), preferred_element_type=F32)


def attend(q, cot, lse, dots, lo, kpos, qpos, kv_ref, kt_ref, src_ref, dst_ref, dkv_ref):
    head_dim, keys = kt_ref.shape
    rows, width = q.shape
    scale = head_dim**-0.5
    key = kpos + lax.broadcasted_iota(jnp.int32, (keys, rows), 0)
    query = qpos + lax.broadcasted_iota(jnp.int32, (1, rows), 1)
    allowed = (key >= lo) & (key <= query)
    lse2 = lse * LOG2E
    k = kv_ref[:, :head_dim]
    v = kv_ref[:, head_dim:]
    dk = jnp.zeros((keys, head_dim), F32)
    dv = jnp.zeros((keys, head_dim), F32)
    for h in range(width // head_dim):
        cols = slice(h * head_dim, (h + 1) * head_dim)
        qh = q[:, cols]
        oh = cot[:, cols]
        scores = dot(k, qh, 1, 1)
        prob_grad = dot(v, oh, 1, 1)
        probs = jnp.where(allowed, jnp.exp2(scores * (scale * LOG2E) - lse2[h : h + 1]), 0.0)
        score_low = (probs * (prob_grad - dots[h : h + 1])).astype(BF16)
        probs_low = probs.astype(BF16)
        dv += dot(probs_low, oh, 1, 0)
        dk += dot(score_low, qh, 1, 0)
        part = dot(kt_ref[...], score_low, 1, 0)
        dst_ref[h] = part if src_ref is None else src_ref[h] + part
    dkv_ref[:, :head_dim] += dk * scale
    dkv_ref[:, head_dim:] += dv


def kernel(names, jobs, *refs):
    r = dict(zip(names, refs))
    marks, kt, dkv = r["marks"], r["kt"], r["dkv"]
    head_dim, keys = kt.shape
    per = keys // ROWS
    chip, core = marks[0], marks[1]
    chip_pos = chip * (2 * keys)
    written = set()
    for back in sorted({back for _, back in jobs}):
        kpos = (chip - back) * (2 * keys) + core * keys
        groups = [who for who, at in jobs if at == back]
        kv_ref = r[f"kv{back}"]
        counts = []
        for who in groups:
            block = core if who == "own" else 1 - core
            count = 0
            for g in range(per):
                count = count + (marks[2 + block * per + g] < kpos + keys).astype(jnp.int32)
            if back == 0:
                count = per if who == "own" else jnp.where(core == 0, count, 0)
            else:
                count = jnp.where(kpos >= 0, count, 0)
            counts.append(count)
        kt[...] = kv_ref[:, :head_dim].T
        first = back == min(at for _, at in jobs)
        dkv[...] = r["dkv_in"][...] if first and "dkv_in" in r else jnp.zeros_like(dkv)
        for who, count in zip(groups, counts):
            block = core if who == "own" else 1 - core
            dst = r[f"acc_out_{who}"]
            src = dst if who in written else r.get(f"acc_in_{who}")
            written.add(who)

            def step(g, unused, who=who, block=block, dst=dst, src=src, kpos=kpos, kv_ref=kv_ref):
                rows = pl.ds(pl.multiple_of(g * ROWS, ROWS), ROWS)
                at = block * per + g
                here = pl.ds(pl.multiple_of(at * ROWS, ROWS), ROWS)
                attend(r[f"q_{who}"].at[rows], r[f"cot_{who}"].at[rows], r[f"lse_{who}"][:, rows],
                       r[f"dots_{who}"][:, rows], r["lo"][0:1, here], kpos, chip_pos + at * ROWS,
                       kv_ref, kt, None if src is None else src.at[g], dst.at[g], dkv)
                return unused

            def skip(g, unused, dst=dst, src=src):
                if src is None:
                    dst[g] = jnp.zeros(dst.shape[1:], F32)
                else:
                    dst[g] = src[g]
                return unused

            lax.fori_loop(0, count, step, 0)
            if src is not dst:
                lax.fori_loop(count, per, skip, 0)
        out = r[f"dkv_out{back}"]
        out[...] = dkv[...].astype(out.dtype)
    if "give" in r:
        r["give"][...] = r["acc_out_other"][...].astype(BF16)
    if "sum_out" in r:
        r["sum_out"][...] = r["sum_in"][...] + r["part"][...].astype(F32)


def far_kernel(names, dists, *refs):
    r = dict(zip(names, refs))
    marks, kt, dkv, kvs = r["marks"], r["kt"], r["dkv"], r["kvs"]
    head_dim, keys = kt.shape
    per = keys // ROWS
    chip, core = marks[0], marks[1]
    chip_pos = chip * (2 * keys)
    dkv[...] = jnp.zeros_like(dkv)
    for who in ("own", "other"):
        r[f"acc_out_{who}"][...] = r[f"acc_in_{who}"][...]
    for n, d in enumerate(dists):
        @pl.when((chip >= d) & (marks[2] < (chip - d) * (2 * keys) + (core + 1) * keys))
        def _():
            kvs[n] = r[f"kv{d}"][...]

    def block_of_keys(n, unused):
        kpos = (chip - (n + dists[0])) * (2 * keys) + core * keys

        @pl.when((kpos >= 0) & (marks[2] < kpos + keys))
        def _():
            kt[...] = kvs[n, :, :head_dim].T
            for who in ("own", "other"):
                block = core if who == "own" else 1 - core
                count = 0
                for g in range(per):
                    count = count + (marks[2 + block * per + g] < kpos + keys).astype(jnp.int32)

                def step(g, unused, who=who, block=block):
                    rows = pl.ds(pl.multiple_of(g * ROWS, ROWS), ROWS)
                    at = block * per + g
                    here = pl.ds(pl.multiple_of(at * ROWS, ROWS), ROWS)
                    dst = r[f"acc_out_{who}"].at[g]
                    attend(r[f"q_{who}"].at[rows], r[f"cot_{who}"].at[rows],
                           r[f"lse_{who}"][:, rows], r[f"dots_{who}"][:, rows], r["lo"][0:1, here],
                           kpos, chip_pos + at * ROWS, kvs.at[n], kt, dst, dst, dkv.at[n])
                    return unused

                lax.fori_loop(0, count, step, 0)

        return unused

    lax.fori_loop(0, len(dists), block_of_keys, 0)
    for n, d in enumerate(dists):
        r[f"dkv_out{d}"][...] = dkv[n].astype(BF16)
    r["give"][...] = r["acc_out_other"][...].astype(BF16)


def finish_kernel(mine_ref, got_ref, out_ref):
    per, heads, head_dim = got_ref.shape[:3]
    scale = head_dim**-0.5
    for g in range(per):
        for h in range(heads):
            part = (mine_ref[g, h] + got_ref[g, h].astype(F32)) * scale
            out_ref[g * ROWS : (g + 1) * ROWS, h * head_dim : (h + 1) * head_dim] = part.T.astype(BF16)


def pack_grads(n_dev, reach, always, q, kv, cot, lse, dots, marks, lo, pack_reach):
    tok, width = q.shape
    head_dim = kv.shape[1] // 2
    heads = width // head_dim
    per = tok // ROWS
    cores = [(i, i ^ 1) for i in range(n_dev)]
    vmem = pl.BlockSpec(memory_space=pltpu.VMEM)
    smem = pl.BlockSpec(memory_space=pltpu.SMEM)
    acc32 = jax.ShapeDtypeStruct((per, heads, head_dim, ROWS), F32)
    acc16 = jax.ShapeDtypeStruct((per, heads, head_dim, ROWS), BF16)
    part32 = jax.ShapeDtypeStruct((tok, 2 * head_dim), F32)
    part16 = jax.ShapeDtypeStruct((tok, 2 * head_dim), BF16)
    tile_flops = 5 * 2 * tok * tok * width

    have = {"marks": marks, "lo": lo, "kv0": kv}
    for name, mine in (("lse", lse), ("dots", dots), ("q", q), ("cot", cot)):
        have[name + "_own"] = mine
        have[name + "_other"] = lax.ppermute(mine, "ctx", cores)
    for d in range(1, reach + 1):
        pairs = [(i, i + 2 * d) for i in range(n_dev - 2 * d)]
        have[f"kv{d}"] = lax.ppermute(kv, "ctx", pairs)

    def call(name, jobs, tiles, extra, outs):
        groups = sorted({who for who, _ in jobs})
        ins = {"marks": marks, "lo": lo}
        for who in groups:
            for part in ("lse", "dots", "q", "cot"):
                ins[f"{part}_{who}"] = have[f"{part}_{who}"]
        for back in sorted({back for _, back in jobs}):
            ins[f"kv{back}"] = have[f"kv{back}"]
        ins.update(extra)
        names = list(ins) + list(outs) + ["kt", "dkv"]
        part = (tok, 2 * head_dim)
        scratch = [pltpu.VMEM((head_dim, tok), BF16), pltpu.VMEM(part, F32)]
        body = functools.partial(kernel, names, jobs)
        if name == "far":
            dists = sorted({back for _, back in jobs})
            names += ["kvs", "acc_out_other"]
            body = functools.partial(far_kernel, names, dists)
            scratch = [scratch[0], pltpu.VMEM((len(dists),) + part, F32), pltpu.VMEM((len(dists),) + part, BF16)]
            scratch.append(pltpu.VMEM(acc32.shape, F32))
        got = pl.pallas_call(
            body,
            out_shape=tuple(outs.values()),
            in_specs=[smem] + [vmem] * (len(ins) - 1),
            out_specs=(vmem,) * len(outs),
            scratch_shapes=scratch,
            compiler_params=pltpu.CompilerParams(vmem_limit_bytes=14 * MIB),
            cost_estimate=pl.CostEstimate(
                flops=int(2 * tiles * tile_flops), bytes_accessed=4 * MIB, transcendentals=0
            ),
            name=name,
        )(*ins.values())
        return dict(zip(outs, got))

    def send(dkv, d):
        return lax.ppermute(dkv, "ctx", [(i + 2 * d, i) for i in range(n_dev - 2 * d)])

    got = call("own", [("own", 0)], 0.2, {}, {"acc_out_own": acc32, "dkv_out0": part32})
    own, total = got["acc_out_own"], got["dkv_out0"]
    got = call(
        "near", [("other", 0), ("own", 1), ("other", 1)], 0.5, {"acc_in_own": own, "dkv_in": total},
        {"acc_out_own": acc32, "acc_out_other": acc32, "dkv_out0": part32, "dkv_out1": part16},
    )
    own, other, total = got["acc_out_own"], got["acc_out_other"], got["dkv_out0"]
    parts = [send(got["dkv_out1"], 1)]

    def adding(extra, outs):
        if len(parts) > 1:
            extra.update(sum_in=total, part=parts.pop(0))
            outs["sum_out"] = part32

    for d in range(2, always + 1):
        extra = {"acc_in_own": own, "acc_in_other": other}
        outs = {"acc_out_own": acc32, "acc_out_other": acc32, f"dkv_out{d}": part16}
        adding(extra, outs)
        got = call(f"back_{d}", [("own", d), ("other", d)], 1, extra, outs)
        own, other, total = got["acc_out_own"], got["acc_out_other"], got.get("sum_out", total)
        parts.append(send(got[f"dkv_out{d}"], d))
    far = range(always + 1, reach + 1)
    extra = {"acc_in_own": own, "acc_in_other": other}
    outs = {"acc_out_own": acc32, "give": acc16}
    outs.update({f"dkv_out{d}": part16 for d in far})
    got = call("far", [(who, d) for d in far for who in ("own", "other")], 1, extra, outs)
    swapped = lax.ppermute(got["give"], "ctx", cores)

    def more(most):
        out = jnp.zeros(part32.shape, F32)
        for d in range(always + 1, most + 1):
            out = out + send(got[f"dkv_out{d}"], d).astype(F32)
        return out

    branches = [functools.partial(more, d) for d in range(always, reach + 1)]
    rest = lax.switch(jnp.clip(pack_reach - always, 0, reach - always), branches)
    grad_q = pl.pallas_call(
        finish_kernel,
        out_shape=jax.ShapeDtypeStruct((tok, width), BF16),
        in_specs=[vmem, vmem],
        out_specs=vmem,
        compiler_params=pltpu.CompilerParams(vmem_limit_bytes=16 * MIB),
        cost_estimate=pl.CostEstimate(flops=2 * MIB, bytes_accessed=4 * MIB, transcendentals=0),
        name="finish",
    )(got["acc_out_own"], swapped)
    grad_kv = total + rest
    for part in parts:
        grad_kv = grad_kv + part.astype(F32)
    return grad_q[None], grad_kv.astype(BF16)[None]


def per_device(n_dev, queries, keys_values, grad_out, log_norms, out_dots, doc_ids):
    tok = queries.shape[1]
    seq = doc_ids.shape[1]
    chip_tok = 2 * tok
    q, kv, cot, lse, dots = queries[0], keys_values[0], grad_out[0], log_norms[0], out_dots[0]
    me = lax.axis_index("ctx").astype(jnp.int32)
    chip, core = me // 2, me % 2
    lo = lax.dynamic_slice_in_dim(doc_ids, chip * chip_tok, chip_tok, 1)
    marks = jnp.concatenate([jnp.stack([chip, core]), lo[0, ::ROWS]])
    most = min(n_dev // 2 - 1, -(-(seq - SPAN - 2) // chip_tok))
    firsts = doc_ids[0, ::chip_tok] // chip_tok
    pack_reach = jnp.max(jnp.arange(n_dev // 2, dtype=jnp.int32) - firsts)
    return pack_grads(n_dev, most, min(3, most), q, kv, cot, lse, dots, marks, lo, pack_reach)


def solution(mesh):
    in_specs = (
        P("pair", "ctx", None),
        P("pair", "ctx", None),
        P("pair", "ctx", None),
        P("pair", None, "ctx"),
        P("pair", None, "ctx"),
        P("pair", None),
    )
    out_specs = (P("pair", "ctx", None), P("pair", "ctx", None))
    return jax.shard_map(
        functools.partial(per_device, mesh.shape["ctx"]),
        mesh=mesh, in_specs=in_specs, out_specs=out_specs, check_vma=False,
    )
```

```python
import functools
import math

import jax
import jax.numpy as jnp
from jax import lax
from jax.experimental import pallas as pl
from jax.experimental.pallas import tpu as pltpu
from jax.sharding import PartitionSpec as P

F32 = jnp.float32
BF16 = jnp.bfloat16
LOG2E = math.log2(math.e)
ROWS = 256
MIB = 1 << 20
SPAN = 2048


def dot(a, b, dim_a, dim_b):
    return lax.dot_general(a, b, (((dim_a,), (dim_b,)), ((), ())), preferred_element_type=F32)


def attend(q, cot, lse, dots, lo, kpos, qpos, kv_ref, kt_ref, src_ref, dst_ref, dkv_ref):
    head_dim, keys = kt_ref.shape
    rows, width = q.shape
    scale = head_dim**-0.5
    key = kpos + lax.broadcasted_iota(jnp.int32, (keys, rows), 0)
    query = qpos + lax.broadcasted_iota(jnp.int32, (1, rows), 1)
    allowed = (key >= lo) & (key <= query)
    lse2 = lse * LOG2E
    k = kv_ref[:, :head_dim]
    v = kv_ref[:, head_dim:]
    dk = jnp.zeros((keys, head_dim), F32)
    dv = jnp.zeros((keys, head_dim), F32)
    for h in range(width // head_dim):
        cols = slice(h * head_dim, (h + 1) * head_dim)
        qh = q[:, cols]
        oh = cot[:, cols]
        scores = dot(k, qh, 1, 1)
        prob_grad = dot(v, oh, 1, 1)
        probs = jnp.where(allowed, jnp.exp2(scores * (scale * LOG2E) - lse2[h : h + 1]), 0.0)
        score_low = (probs * (prob_grad - dots[h : h + 1])).astype(BF16)
        probs_low = probs.astype(BF16)
        dv += dot(probs_low, oh, 1, 0)
        dk += dot(score_low, qh, 1, 0)
        part = dot(kt_ref[...], score_low, 1, 0)
        dst_ref[h] = part if src_ref is None else src_ref[h] + part
    dkv_ref[:, :head_dim] += dk * scale
    dkv_ref[:, head_dim:] += dv


def kernel(names, jobs, *refs):
    r = dict(zip(names, refs))
    marks, kt, dkv = r["marks"], r["kt"], r["dkv"]
    head_dim, keys = kt.shape
    per = keys // ROWS
    chip, core = marks[0], marks[1]
    chip_pos = chip * (2 * keys)
    written = set()
    for back in sorted({back for _, back in jobs}):
        kpos = (chip - back) * (2 * keys) + core * keys
        groups = [who for who, at in jobs if at == back]
        kv_ref = r[f"kv{back}"]
        counts = []
        for who in groups:
            block = core if who == "own" else 1 - core
            count = 0
            for g in range(per):
                count = count + (marks[2 + block * per + g] < kpos + keys).astype(jnp.int32)
            if back == 0:
                count = per if who == "own" else jnp.where(core == 0, count, 0)
            else:
                count = jnp.where(kpos >= 0, count, 0)
            counts.append(count)
        kt[...] = kv_ref[:, :head_dim].T
        first = back == min(at for _, at in jobs)
        dkv[...] = r["dkv_in"][...] if first and "dkv_in" in r else jnp.zeros_like(dkv)
        for who, count in zip(groups, counts):
            block = core if who == "own" else 1 - core
            dst = r[f"acc_out_{who}"]
            src = dst if who in written else r.get(f"acc_in_{who}")
            written.add(who)

            def step(g, unused, who=who, block=block, dst=dst, src=src, kpos=kpos, kv_ref=kv_ref):
                rows = pl.ds(pl.multiple_of(g * ROWS, ROWS), ROWS)
                at = block * per + g
                here = pl.ds(pl.multiple_of(at * ROWS, ROWS), ROWS)
                attend(r[f"q_{who}"].at[rows], r[f"cot_{who}"].at[rows], r[f"lse_{who}"][:, rows],
                       r[f"dots_{who}"][:, rows], r["lo"][0:1, here], kpos, chip_pos + at * ROWS,
                       kv_ref, kt, None if src is None else src.at[g], dst.at[g], dkv)
                return unused

            def skip(g, unused, dst=dst, src=src):
                if src is None:
                    dst[g] = jnp.zeros(dst.shape[1:], F32)
                else:
                    dst[g] = src[g]
                return unused

            lax.fori_loop(0, count, step, 0)
            if src is not dst:
                lax.fori_loop(count, per, skip, 0)
        out = r[f"dkv_out{back}"]
        out[...] = dkv[...].astype(out.dtype)
    if "give" in r:
        r["give"][...] = r["acc_out_other"][...].astype(BF16)
    if "sum_out" in r:
        r["sum_out"][...] = r["sum_in"][...] + r["part"][...].astype(F32)


def far_kernel(names, dists, *refs):
    r = dict(zip(names, refs))
    marks, kt, dkv, kvs = r["marks"], r["kt"], r["dkv"], r["kvs"]
    head_dim, keys = kt.shape
    per = keys // ROWS
    chip, core = marks[0], marks[1]
    chip_pos = chip * (2 * keys)
    dkv[...] = jnp.zeros_like(dkv)
    for who in ("own", "other"):
        r[f"acc_out_{who}"][...] = r[f"acc_in_{who}"][...]
    for n, d in enumerate(dists):
        @pl.when((chip >= d) & (marks[2] < (chip - d) * (2 * keys) + (core + 1) * keys))
        def _():
            kvs[n] = r[f"kv{d}"][...]

    def block_of_keys(n, unused):
        kpos = (chip - (n + dists[0])) * (2 * keys) + core * keys

        @pl.when((kpos >= 0) & (marks[2] < kpos + keys))
        def _():
            kt[...] = kvs[n, :, :head_dim].T
            for who in ("own", "other"):
                block = core if who == "own" else 1 - core
                count = 0
                for g in range(per):
                    count = count + (marks[2 + block * per + g] < kpos + keys).astype(jnp.int32)

                def step(g, unused, who=who, block=block):
                    rows = pl.ds(pl.multiple_of(g * ROWS, ROWS), ROWS)
                    at = block * per + g
                    here = pl.ds(pl.multiple_of(at * ROWS, ROWS), ROWS)
                    dst = r[f"acc_out_{who}"].at[g]
                    attend(r[f"q_{who}"].at[rows], r[f"cot_{who}"].at[rows],
                           r[f"lse_{who}"][:, rows], r[f"dots_{who}"][:, rows], r["lo"][0:1, here],
                           kpos, chip_pos + at * ROWS, kvs.at[n], kt, dst, dst, dkv.at[n])
                    return unused

                lax.fori_loop(0, count, step, 0)

        return unused

    lax.fori_loop(0, len(dists), block_of_keys, 0)
    for n, d in enumerate(dists):
        r[f"dkv_out{d}"][...] = dkv[n].astype(BF16)
    r["give"][...] = r["acc_out_other"][...].astype(BF16)
    if "sum_out" in r:
        r["sum_out"][...] = r["sum_in"][...] + r["part"][...].astype(F32)


def finish_kernel(mine_ref, got_ref, *refs):
    *part_refs, out_ref, kv_ref = refs
    total = part_refs[0][...]
    for ref in part_refs[1:]:
        total = total + ref[...].astype(F32)
    kv_ref[...] = total.astype(BF16)
    per, heads, head_dim = got_ref.shape[:3]
    scale = head_dim**-0.5
    for g in range(per):
        for h in range(heads):
            part = (mine_ref[g, h] + got_ref[g, h].astype(F32)) * scale
            out_ref[g * ROWS : (g + 1) * ROWS, h * head_dim : (h + 1) * head_dim] = part.T.astype(BF16)


def pack_grads(n_dev, reach, always, q, kv, cot, lse, dots, marks, lo, pack_reach):
    tok, width = q.shape
    head_dim = kv.shape[1] // 2
    heads = width // head_dim
    per = tok // ROWS
    cores = [(i, i ^ 1) for i in range(n_dev)]
    vmem = pl.BlockSpec(memory_space=pltpu.VMEM)
    smem = pl.BlockSpec(memory_space=pltpu.SMEM)
    acc32 = jax.ShapeDtypeStruct((per, heads, head_dim, ROWS), F32)
    acc16 = jax.ShapeDtypeStruct((per, heads, head_dim, ROWS), BF16)
    part32 = jax.ShapeDtypeStruct((tok, 2 * head_dim), F32)
    part16 = jax.ShapeDtypeStruct((tok, 2 * head_dim), BF16)
    tile_flops = 5 * 2 * tok * tok * width

    have = {"marks": marks, "lo": lo, "kv0": kv}
    for name, mine in (("lse", lse), ("dots", dots), ("q", q), ("cot", cot)):
        have[name + "_own"] = mine
        have[name + "_other"] = lax.ppermute(mine, "ctx", cores)
    for d in range(1, reach + 1):
        pairs = [(i, i + 2 * d) for i in range(n_dev - 2 * d)]
        have[f"kv{d}"] = lax.ppermute(kv, "ctx", pairs)

    def call(name, jobs, tiles, extra, outs):
        groups = sorted({who for who, _ in jobs})
        ins = {"marks": marks, "lo": lo}
        for who in groups:
            for part in ("lse", "dots", "q", "cot"):
                ins[f"{part}_{who}"] = have[f"{part}_{who}"]
        for back in sorted({back for _, back in jobs}):
            ins[f"kv{back}"] = have[f"kv{back}"]
        ins.update(extra)
        names = list(ins) + list(outs) + ["kt", "dkv"]
        part = (tok, 2 * head_dim)
        scratch = [pltpu.VMEM((head_dim, tok), BF16), pltpu.VMEM(part, F32)]
        body = functools.partial(kernel, names, jobs)
        if name == "far":
            dists = sorted({back for _, back in jobs})
            names += ["kvs", "acc_out_other"]
            body = functools.partial(far_kernel, names, dists)
            scratch = [scratch[0], pltpu.VMEM((len(dists),) + part, F32), pltpu.VMEM((len(dists),) + part, BF16)]
            scratch.append(pltpu.VMEM(acc32.shape, F32))
        got = pl.pallas_call(
            body,
            out_shape=tuple(outs.values()),
            in_specs=[smem] + [vmem] * (len(ins) - 1),
            out_specs=(vmem,) * len(outs),
            scratch_shapes=scratch,
            compiler_params=pltpu.CompilerParams(vmem_limit_bytes=14 * MIB),
            cost_estimate=pl.CostEstimate(
                flops=int(2 * tiles * tile_flops), bytes_accessed=4 * MIB, transcendentals=0
            ),
            name=name,
        )(*ins.values())
        return dict(zip(outs, got))

    def send(dkv, d):
        return lax.ppermute(dkv, "ctx", [(i + 2 * d, i) for i in range(n_dev - 2 * d)])

    got = call("own", [("own", 0)], 0.2, {}, {"acc_out_own": acc32, "dkv_out0": part32})
    own, total = got["acc_out_own"], got["dkv_out0"]
    got = call(
        "near", [("other", 0), ("own", 1), ("other", 1)], 0.5, {"acc_in_own": own, "dkv_in": total},
        {"acc_out_own": acc32, "acc_out_other": acc32, "dkv_out0": part32, "dkv_out1": part16},
    )
    own, other, total = got["acc_out_own"], got["acc_out_other"], got["dkv_out0"]
    parts = [send(got["dkv_out1"], 1)]

    def adding(extra, outs):
        if len(parts) > 1:
            extra.update(sum_in=total, part=parts.pop(0))
            outs["sum_out"] = part32

    for d in range(2, always + 1):
        extra = {"acc_in_own": own, "acc_in_other": other}
        outs = {"acc_out_own": acc32, "acc_out_other": acc32, f"dkv_out{d}": part16}
        adding(extra, outs)
        got = call(f"back_{d}", [("own", d), ("other", d)], 1, extra, outs)
        own, other, total = got["acc_out_own"], got["acc_out_other"], got.get("sum_out", total)
        parts.append(send(got[f"dkv_out{d}"], d))
    far = range(always + 1, reach + 1)
    extra = {"acc_in_own": own, "acc_in_other": other}
    outs = {"acc_out_own": acc32, "give": acc16}
    outs.update({f"dkv_out{d}": part16 for d in far})
    adding(extra, outs)
    got = call("far", [(who, d) for d in far for who in ("own", "other")], 1, extra, outs)
    total = got.get("sum_out", total)
    swapped = lax.ppermute(got["give"], "ctx", cores)

    def more(most):
        out = jnp.zeros(part32.shape, F32)
        for d in range(always + 1, most + 1):
            out = out + send(got[f"dkv_out{d}"], d).astype(F32)
        return out

    branches = [functools.partial(more, d) for d in range(always, reach + 1)]
    rest = lax.switch(jnp.clip(pack_reach - always, 0, reach - always), branches)
    parts = [total, rest] + parts
    grad_q, grad_kv = pl.pallas_call(
        finish_kernel,
        out_shape=(jax.ShapeDtypeStruct((tok, width), BF16), part16),
        in_specs=[vmem] * (2 + len(parts)),
        out_specs=(vmem, vmem),
        compiler_params=pltpu.CompilerParams(vmem_limit_bytes=16 * MIB),
        cost_estimate=pl.CostEstimate(flops=2 * MIB, bytes_accessed=4 * MIB, transcendentals=0),
        name="finish",
    )(got["acc_out_own"], swapped, *parts)
    return grad_q[None], grad_kv[None]


def per_device(n_dev, queries, keys_values, grad_out, log_norms, out_dots, doc_ids):
    tok = queries.shape[1]
    seq = doc_ids.shape[1]
    chip_tok = 2 * tok
    q, kv, cot, lse, dots = queries[0], keys_values[0], grad_out[0], log_norms[0], out_dots[0]
    me = lax.axis_index("ctx").astype(jnp.int32)
    chip, core = me // 2, me % 2
    lo = lax.dynamic_slice_in_dim(doc_ids, chip * chip_tok, chip_tok, 1)
    marks = jnp.concatenate([jnp.stack([chip, core]), lo[0, ::ROWS]])
    most = min(n_dev // 2 - 1, -(-(seq - SPAN - 2) // chip_tok))
    firsts = doc_ids[0, ::chip_tok] // chip_tok
    pack_reach = jnp.max(jnp.arange(n_dev // 2, dtype=jnp.int32) - firsts)
    return pack_grads(n_dev, most, min(3, most), q, kv, cot, lse, dots, marks, lo, pack_reach)


def solution(mesh):
    in_specs = (
        P("pair", "ctx", None),
        P("pair", "ctx", None),
        P("pair", "ctx", None),
        P("pair", None, "ctx"),
        P("pair", None, "ctx"),
        P("pair", None),
    )
    out_specs = (P("pair", "ctx", None), P("pair", "ctx", None))
    return jax.shard_map(
        functools.partial(per_device, mesh.shape["ctx"]),
        mesh=mesh, in_specs=in_specs, out_specs=out_specs, check_vma=False,
    )
```

```python
import functools
import math

import jax
import jax.numpy as jnp
from jax import lax
from jax.experimental import pallas as pl
from jax.experimental.pallas import tpu as pltpu
from jax.sharding import PartitionSpec as P

F32 = jnp.float32
BF16 = jnp.bfloat16
LOG2E = math.log2(math.e)
ROWS = 256
MIB = 1 << 20
SPAN = 2048


def dot(a, b, dim_a, dim_b):
    return lax.dot_general(a, b, (((dim_a,), (dim_b,)), ((), ())), preferred_element_type=F32)


def attend(q, cot, lse, dots, lo, kpos, qpos, kv_ref, kt_ref, src_ref, dst_ref, dkv_ref):
    head_dim, keys = kt_ref.shape
    rows, width = q.shape
    scale = head_dim**-0.5
    key = kpos + lax.broadcasted_iota(jnp.int32, (keys, rows), 0)
    query = qpos + lax.broadcasted_iota(jnp.int32, (1, rows), 1)
    allowed = (key >= lo) & (key <= query)
    lse2 = lse * LOG2E
    k = kv_ref[:, :head_dim]
    v = kv_ref[:, head_dim:]
    dk = jnp.zeros((keys, head_dim), F32)
    dv = jnp.zeros((keys, head_dim), F32)
    for h in range(width // head_dim):
        cols = slice(h * head_dim, (h + 1) * head_dim)
        qh = q[:, cols]
        oh = cot[:, cols]
        scores = dot(k, qh, 1, 1)
        prob_grad = dot(v, oh, 1, 1)
        probs = jnp.where(allowed, jnp.exp2(scores * (scale * LOG2E) - lse2[h : h + 1]), 0.0)
        score_low = (probs * (prob_grad - dots[h : h + 1])).astype(BF16)
        probs_low = probs.astype(BF16)
        dv += dot(probs_low, oh, 1, 0)
        dk += dot(score_low, qh, 1, 0)
        part = dot(kt_ref[...], score_low, 1, 0)
        dst_ref[h] = part if src_ref is None else src_ref[h] + part
    dkv_ref[:, :head_dim] += dk * scale
    dkv_ref[:, head_dim:] += dv


def kernel(names, jobs, *refs):
    r = dict(zip(names, refs))
    marks, kt, dkv = r["marks"], r["kt"], r["dkv"]
    head_dim, keys = kt.shape
    per = keys // ROWS
    chip, core = marks[0], marks[1]
    chip_pos = chip * (2 * keys)
    written = set()
    for back in sorted({back for _, back in jobs}):
        kpos = (chip - back) * (2 * keys) + core * keys
        groups = [who for who, at in jobs if at == back]
        kv_ref = r[f"kv{back}"]
        counts = []
        for who in groups:
            block = core if who == "own" else 1 - core
            count = 0
            for g in range(per):
                count = count + (marks[2 + block * per + g] < kpos + keys).astype(jnp.int32)
            if back == 0:
                count = per if who == "own" else jnp.where(core == 0, count, 0)
            else:
                count = jnp.where(kpos >= 0, count, 0)
            counts.append(count)
        kt[...] = kv_ref[:, :head_dim].T
        first = back == min(at for _, at in jobs)
        dkv[...] = r["dkv_in"][...] if first and "dkv_in" in r else jnp.zeros_like(dkv)
        for who, count in zip(groups, counts):
            block = core if who == "own" else 1 - core
            dst = r[f"acc_out_{who}"]
            src = dst if who in written else r.get(f"acc_in_{who}")
            written.add(who)

            def step(g, unused, who=who, block=block, dst=dst, src=src, kpos=kpos, kv_ref=kv_ref):
                rows = pl.ds(pl.multiple_of(g * ROWS, ROWS), ROWS)
                at = block * per + g
                here = pl.ds(pl.multiple_of(at * ROWS, ROWS), ROWS)
                attend(r[f"q_{who}"].at[rows], r[f"cot_{who}"].at[rows], r[f"lse_{who}"][:, rows],
                       r[f"dots_{who}"][:, rows], r["lo"][0:1, here], kpos, chip_pos + at * ROWS,
                       kv_ref, kt, None if src is None else src.at[g], dst.at[g], dkv)
                return unused

            def skip(g, unused, dst=dst, src=src):
                if src is None:
                    dst[g] = jnp.zeros(dst.shape[1:], F32)
                else:
                    dst[g] = src[g]
                return unused

            lax.fori_loop(0, count, step, 0)
            if src is not dst:
                lax.fori_loop(count, per, skip, 0)
        out = r[f"dkv_out{back}"]
        out[...] = dkv[...].astype(out.dtype)
    if "give" in r:
        r["give"][...] = r["acc_out_other"][...].astype(BF16)
    if "sum_out" in r:
        r["sum_out"][...] = r["sum_in"][...] + r["part"][...].astype(F32)


def far_kernel(names, dists, *refs):
    r = dict(zip(names, refs))
    marks, kt, dkv, kvs = r["marks"], r["kt"], r["dkv"], r["kvs"]
    head_dim, keys = kt.shape
    per = keys // ROWS
    chip, core = marks[0], marks[1]
    chip_pos = chip * (2 * keys)
    dkv[...] = jnp.zeros_like(dkv)
    for who in ("own", "other"):
        r[f"acc_out_{who}"][...] = r[f"acc_in_{who}"][...]
    for n, d in enumerate(dists):
        @pl.when((chip >= d) & (marks[2] < (chip - d) * (2 * keys) + (core + 1) * keys))
        def _():
            kvs[n] = r[f"kv{d}"][...]

    def block_of_keys(n, unused):
        kpos = (chip - (n + dists[0])) * (2 * keys) + core * keys

        @pl.when((kpos >= 0) & (marks[2] < kpos + keys))
        def _():
            kt[...] = kvs[n, :, :head_dim].T
            for who in ("own", "other"):
                block = core if who == "own" else 1 - core
                count = 0
                for g in range(per):
                    count = count + (marks[2 + block * per + g] < kpos + keys).astype(jnp.int32)

                def step(g, unused, who=who, block=block):
                    rows = pl.ds(pl.multiple_of(g * ROWS, ROWS), ROWS)
                    at = block * per + g
                    here = pl.ds(pl.multiple_of(at * ROWS, ROWS), ROWS)
                    dst = r[f"acc_out_{who}"].at[g]
                    attend(r[f"q_{who}"].at[rows], r[f"cot_{who}"].at[rows],
                           r[f"lse_{who}"][:, rows], r[f"dots_{who}"][:, rows], r["lo"][0:1, here],
                           kpos, chip_pos + at * ROWS, kvs.at[n], kt, dst, dst, dkv.at[n])
                    return unused

                lax.fori_loop(0, count, step, 0)

        return unused

    lax.fori_loop(0, len(dists), block_of_keys, 0)
    for n, d in enumerate(dists):
        r[f"dkv_out{d}"][...] = dkv[n].astype(BF16)
    r["give"][...] = r["acc_out_other"][...].astype(BF16)


def finish_kernel(mine_ref, got_ref, *refs):
    *part_refs, out_ref, kv_ref = refs
    total = part_refs[0][...]
    for ref in part_refs[1:]:
        total = total + ref[...].astype(F32)
    kv_ref[...] = total.astype(BF16)
    per, heads, head_dim = got_ref.shape[:3]
    scale = head_dim**-0.5
    for g in range(per):
        for h in range(heads):
            part = (mine_ref[g, h] + got_ref[g, h].astype(F32)) * scale
            out_ref[g * ROWS : (g + 1) * ROWS, h * head_dim : (h + 1) * head_dim] = part.T.astype(BF16)


def pack_grads(n_dev, reach, always, q, kv, cot, lse, dots, marks, lo, pack_reach):
    tok, width = q.shape
    head_dim = kv.shape[1] // 2
    heads = width // head_dim
    per = tok // ROWS
    cores = [(i, i ^ 1) for i in range(n_dev)]
    vmem = pl.BlockSpec(memory_space=pltpu.VMEM)
    smem = pl.BlockSpec(memory_space=pltpu.SMEM)
    acc32 = jax.ShapeDtypeStruct((per, heads, head_dim, ROWS), F32)
    acc16 = jax.ShapeDtypeStruct((per, heads, head_dim, ROWS), BF16)
    part32 = jax.ShapeDtypeStruct((tok, 2 * head_dim), F32)
    part16 = jax.ShapeDtypeStruct((tok, 2 * head_dim), BF16)
    tile_flops = 5 * 2 * tok * tok * width

    have = {"marks": marks, "lo": lo, "kv0": kv}
    for name, mine in (("lse", lse), ("dots", dots), ("q", q), ("cot", cot)):
        have[name + "_own"] = mine
        have[name + "_other"] = lax.ppermute(mine, "ctx", cores)
    for d in range(1, reach + 1):
        pairs = [(i, i + 2 * d) for i in range(n_dev - 2 * d)]
        have[f"kv{d}"] = lax.ppermute(kv, "ctx", pairs)

    def call(name, jobs, tiles, extra, outs):
        groups = sorted({who for who, _ in jobs})
        ins = {"marks": marks, "lo": lo}
        for who in groups:
            for part in ("lse", "dots", "q", "cot"):
                ins[f"{part}_{who}"] = have[f"{part}_{who}"]
        for back in sorted({back for _, back in jobs}):
            ins[f"kv{back}"] = have[f"kv{back}"]
        ins.update(extra)
        names = list(ins) + list(outs) + ["kt", "dkv"]
        part = (tok, 2 * head_dim)
        scratch = [pltpu.VMEM((head_dim, tok), BF16), pltpu.VMEM(part, F32)]
        body = functools.partial(kernel, names, jobs)
        if name == "far":
            dists = sorted({back for _, back in jobs})
            names += ["kvs", "acc_out_other"]
            body = functools.partial(far_kernel, names, dists)
            scratch = [scratch[0], pltpu.VMEM((len(dists),) + part, F32), pltpu.VMEM((len(dists),) + part, BF16)]
            scratch.append(pltpu.VMEM(acc32.shape, F32))
        got = pl.pallas_call(
            body,
            out_shape=tuple(outs.values()),
            in_specs=[smem] + [vmem] * (len(ins) - 1),
            out_specs=(vmem,) * len(outs),
            scratch_shapes=scratch,
            compiler_params=pltpu.CompilerParams(vmem_limit_bytes=14 * MIB),
            cost_estimate=pl.CostEstimate(
                flops=int(2 * tiles * tile_flops), bytes_accessed=4 * MIB, transcendentals=0
            ),
            name=name,
        )(*ins.values())
        return dict(zip(outs, got))

    def send(dkv, d):
        return lax.ppermute(dkv, "ctx", [(i + 2 * d, i) for i in range(n_dev - 2 * d)])

    got = call("own", [("own", 0)], 0.2, {}, {"acc_out_own": acc32, "dkv_out0": part32})
    own, total = got["acc_out_own"], got["dkv_out0"]
    got = call(
        "near", [("other", 0), ("own", 1), ("other", 1)], 0.5, {"acc_in_own": own, "dkv_in": total},
        {"acc_out_own": acc32, "acc_out_other": acc32, "dkv_out0": part32, "dkv_out1": part16},
    )
    own, other, total = got["acc_out_own"], got["acc_out_other"], got["dkv_out0"]
    parts = [send(got["dkv_out1"], 1)]

    def adding(extra, outs):
        if len(parts) > 1:
            extra.update(sum_in=total, part=parts.pop(0))
            outs["sum_out"] = part32

    for d in range(2, always + 1):
        extra = {"acc_in_own": own, "acc_in_other": other}
        outs = {"acc_out_own": acc32, "acc_out_other": acc32, f"dkv_out{d}": part16}
        adding(extra, outs)
        got = call(f"back_{d}", [("own", d), ("other", d)], 1, extra, outs)
        own, other, total = got["acc_out_own"], got["acc_out_other"], got.get("sum_out", total)
        parts.append(send(got[f"dkv_out{d}"], d))
    far = range(always + 1, reach + 1)
    extra = {"acc_in_own": own, "acc_in_other": other}
    outs = {"acc_out_own": acc32, "give": acc16}
    outs.update({f"dkv_out{d}": part16 for d in far})
    got = call("far", [(who, d) for d in far for who in ("own", "other")], 1, extra, outs)
    swapped = lax.ppermute(got["give"], "ctx", cores)

    def more(most):
        out = jnp.zeros(part32.shape, F32)
        for d in range(always + 1, most + 1):
            out = out + send(got[f"dkv_out{d}"], d).astype(F32)
        return out

    branches = [functools.partial(more, d) for d in range(always, reach + 1)]
    rest = lax.switch(jnp.clip(pack_reach - always, 0, reach - always), branches)
    parts = [total, rest] + parts
    grad_q, grad_kv = pl.pallas_call(
        finish_kernel,
        out_shape=(jax.ShapeDtypeStruct((tok, width), BF16), part16),
        in_specs=[vmem] * (2 + len(parts)),
        out_specs=(vmem, vmem),
        compiler_params=pltpu.CompilerParams(vmem_limit_bytes=16 * MIB),
        cost_estimate=pl.CostEstimate(flops=2 * MIB, bytes_accessed=4 * MIB, transcendentals=0),
        name="finish",
    )(got["acc_out_own"], swapped, *parts)
    return grad_q[None], grad_kv[None]


def per_device(n_dev, queries, keys_values, grad_out, log_norms, out_dots, doc_ids):
    tok = queries.shape[1]
    seq = doc_ids.shape[1]
    chip_tok = 2 * tok
    q, kv, cot, lse, dots = queries[0], keys_values[0], grad_out[0], log_norms[0], out_dots[0]
    me = lax.axis_index("ctx").astype(jnp.int32)
    chip, core = me // 2, me % 2
    lo = lax.dynamic_slice_in_dim(doc_ids, chip * chip_tok, chip_tok, 1)
    marks = jnp.concatenate([jnp.stack([chip, core]), lo[0, ::ROWS]])
    most = min(n_dev // 2 - 1, -(-(seq - SPAN - 2) // chip_tok))
    firsts = doc_ids[0, ::chip_tok] // chip_tok
    pack_reach = jnp.max(jnp.arange(n_dev // 2, dtype=jnp.int32) - firsts)
    return pack_grads(n_dev, most, min(3, most), q, kv, cot, lse, dots, marks, lo, pack_reach)


def solution(mesh):
    in_specs = (
        P("pair", "ctx", None),
        P("pair", "ctx", None),
        P("pair", "ctx", None),
        P("pair", None, "ctx"),
        P("pair", None, "ctx"),
        P("pair", None),
    )
    out_specs = (P("pair", "ctx", None), P("pair", "ctx", None))
    return jax.shard_map(
        functools.partial(per_device, mesh.shape["ctx"]),
        mesh=mesh, in_specs=in_specs, out_specs=out_specs, check_vma=False,
    )
```
